512 devices in a mesh: row: 16 (over x, y_hi), col: 16 (over y_lo, z), img: 2 (over core).
Axes of the slice: x: 4, y: 8 (y_hi: 4, y_lo: 2; y = y_hi * 2 + y_lo), z: 8, core: 2. Of those that a mesh axis runs over, the one named last changes fastest.
Arguments:
- student: bfloat16 [2, 4096, 4096], P('img', 'col', 'row'), may hold values from -6 to 6
- teacher: bfloat16 [2, 4096, 4096], P('img', 'col', 'row'), may hold values from -6 to 6
Outputs:
- feature_grad: bfloat16 [2, 4096, 4096], P('img', 'col', 'row')
The draws below stay inside these ranges and needn't reach their ends.
All inputs are finite; a program needn't handle non-finite values.
Results may differ from the reference program's by a relative error of at most 0.012.
Values may be sent and summed in bfloat16 or wider, within the bound.
A program may use at most 64 MiB of HBM per device.

```python
import jax
import jax.numpy as jnp
from jax import lax

D = 4096
PB = 256
PATCHES = 4096
IMAGES = 2
N_COL = 16


def levels(key, dims, shards, low, largest):
    def one(axis_at, shards_of):
        heights = jax.random.uniform(jax.random.fold_in(jax.random.fold_in(key, 6), axis_at), (shards_of,), jnp.float32, low / len(shards), largest / len(shards))
        return jnp.repeat(jnp.exp(heights), dims[axis_at] // shards_of).reshape((-1,) + (1,) * (len(dims) - axis_at - 1))

    factor_of = one(*shards[0])
    for cut in shards[1:]:
        factor_of = factor_of * one(*cut)
    return factor_of


def scatter_about(stream_key, dims, scale, most, shards=(), held_as=jnp.bfloat16):
    values = scale * jax.random.normal(stream_key, dims, jnp.float32)
    if shards:
        values = values * levels(stream_key, dims, shards, -0.22, 0.18)
    return jnp.clip(values, -most, most).astype(held_as)


def setup_inputs(seed: int = 0) -> dict:
    key_of = jax.random.split(jax.random.key(seed), 3)
    return {
        "student": scatter_about(key_of[0], (IMAGES, PATCHES, D), 1.0, 6.0, ((0, 2), (1, 16), (2, 16))),
        "teacher": scatter_about(key_of[1], (IMAGES, PATCHES, D), 1.0, 6.0, ((0, 2), (1, 16), (2, 16))),
    }


def one_image(pair):
    xs, xt = pair
    xs32 = xs.astype(jnp.float32)
    xt32 = xt.astype(jnp.float32)
    gram_student = jnp.dot(xs32, xs32.T) / D
    gram_teacher = jnp.dot(xt32, xt32.T) / D
    gap = (gram_student - gram_teacher).astype(jnp.bfloat16).astype(jnp.float32)
    gap_rows = gap.reshape(N_COL, PB, PB * N_COL)
    feat_rows = xs32.reshape(N_COL, PB, D)

    def accumulate(total, blocks):
        gap_block, feat_block = blocks
        part = jnp.dot(gap_block.T, feat_block).astype(jnp.bfloat16)
        return total + part.astype(jnp.float32), None

    total, unused = lax.scan(accumulate, jnp.zeros((PB * N_COL, D), jnp.float32), (gap_rows, feat_rows))
    return total.astype(jnp.bfloat16)


def reference(student, teacher):
    return lax.map(one_image, (student, teacher))
```

```python
import functools

import jax
import jax.numpy as jnp
from jax import lax
from jax.experimental import pallas as pl
from jax.experimental.pallas import tpu as pltpu
from jax.sharding import PartitionSpec as P

MESH = pl.DeviceIdType.MESH
F32, BF16 = jnp.float32, jnp.bfloat16

COVER = ((0, 0), (0, 1), (0, -2), (1, 2), (1, -2))
CHUNKS = (
    ((0, 0, 256),),
    ((0, 1, 256), (0, 2, 256), (1, 2, 256)),
    ((0, 3, 256), (1, 3, 256), (2, 3, 128)),
    ((1, 4, 256), (2, 4, 128), (3, 4, 128)),
)
WIDTH = sum(w for chunk in CHUNKS for _, _, w in chunk)
COPIES = 8 + 4 + 12 * len(CHUNKS)


def dot(a, b, dims):
    return lax.dot_general(a, b, (dims, ((), ())), preferred_element_type=F32)


def kernel(scale, s_ref, t_ref, out_ref, sb, tb, gs, gf, rx, xs, xf, ry, gg, half, ps, fr, send, recv):
    r, c, img = lax.axis_index("row"), lax.axis_index("col"), lax.axis_index("img")
    x, h, l, z = r // 4, r % 4, c // 8, c % 8
    way = 1 - 2 * img

    def device(dx=0, dh=0, dl=0, dz=0):
        return (
            (x + dx) % 4 * 4 + (h + dh) % 4,
            (l + dl) % 2 * 8 + (z + 8 + way * dz) % 8,
            img,
        )

    count = [0]
    started = []

    def copy(src, dst, to):
        k = count[0]
        count[0] += 1
        made = pltpu.make_async_remote_copy(
            src_ref=src, dst_ref=dst, send_sem=send.at[k], recv_sem=recv.at[k],
            device_id=to, device_id_type=MESH,
        )
        made.start()
        started.append(made)
        return made

    peers = [device(dl=a, dz=b) for a, b in ((0, 1), (0, -2), (1, 1), (1, 0), (0, -1), (0, 2), (1, -2), (1, 2))]
    peers += [device(dx=k) for k in (1, 2, 3)] + [device(dh=k) for k in (1, 2, 3)]
    barrier = pltpu.get_barrier_semaphore()
    for peer in peers:
        pl.semaphore_signal(barrier, inc=1, device_id=peer, device_id_type=MESH)
    pl.semaphore_wait(barrier, len(peers))

    def slot(which, k):
        own, held = ((s_ref, sb), (t_ref, tb))[which]
        return own.at[0] if k == 0 else held.at[k - 1]

    got = {}
    for which in (0, 1):
        got[which, 1] = copy(slot(which, 0), slot(which, 1), device(dz=-1))
        got[which, 2] = copy(slot(which, 0), slot(which, 2), device(dz=2))

    def forward(which):
        got[which, 1].wait_recv()
        got[which, 3] = copy(slot(which, 1), slot(which, 3), device(dl=1, dz=-1))
        got[which, 2].wait_recv()
        got[which, 4] = copy(slot(which, 2), slot(which, 4), device(dl=1))

    def halved(i, j):
        first = (z < 4) if COVER[i][0] == COVER[j][0] else (l == 0)
        f = jnp.where(first, 1, 0)
        rows, columns = i * f + j * (1 - f), j * f + i * (1 - f)
        return rows, columns, pl.multiple_of((1 - f) * 128, 128)

    columns_of = {}
    spans = []
    at = 0
    for chunk in CHUNKS:
        begin = at
        for i, j, w in chunk:
            columns_of[i, j] = pl.ds(at, w)
            at += w
        spans.append(pl.ds(begin, at - begin))

    def gram(n):
        for i, j, w in CHUNKS[n]:
            if w == 256:
                a_s, b_s, a_t, b_t = slot(0, i)[...], slot(0, j)[...], slot(1, i)[...], slot(1, j)[...]
            else:
                rows, columns, begin = halved(i, j)
                a_s, a_t = sb[rows - 1], tb[rows - 1]
                b_s, b_t = sb[columns - 1, pl.ds(begin, 128)], tb[columns - 1, pl.ds(begin, 128)]
            part = (dot(a_s, b_s, ((1,), (1,))) - dot(a_t, b_t, ((1,), (1,)))) * scale
            gf[:, columns_of[i, j]] = part
            gs[:, columns_of[i, j]] = part.astype(BF16)
        for k in (2, 1, 3):
            rows = pl.multiple_of((x + k) % 4 * 64, 64)
            got["sx", n, k] = copy(gs.at[pl.ds(rows, 64), spans[n]], rx.at[k - 1, :, spans[n]], device(dx=k))

    own_x = pl.multiple_of(x * 64, 64)
    own_y = pl.multiple_of(h * 16, 16)
    own = pl.multiple_of(x * 64 + h * 16, 16)

    def sum_x(n):
        for k in (1, 3, 2):
            got["sx", n, k].wait_recv()
        total = gf[pl.ds(own_x, 64), spans[n]]
        for k in range(3):
            total += rx[k, :, spans[n]].astype(F32)
        xf[:, spans[n]] = total
        xs[:, spans[n]] = total.astype(BF16)
        for k in (2, 1, 3):
            rows = pl.multiple_of((h + k) % 4 * 16, 16)
            got["sy", n, k] = copy(xs.at[pl.ds(rows, 16), spans[n]], ry.at[k - 1, :, spans[n]], device(dh=k))

    def sum_y(n):
        for k in (1, 3, 2):
            got["sy", n, k].wait_recv()
        total = xf[pl.ds(own_y, 16), spans[n]]
        for k in range(3):
            total += ry[k, :, spans[n]].astype(F32)
        gg[pl.ds(own, 16), spans[n]] = total.astype(BF16)
        for k in (2, 1, 3):
            piece = gg.at[pl.ds(own, 16), spans[n]]
            got["gy", n, k] = copy(piece, piece, device(dh=k))

    def gather_x(n):
        for k in (1, 3, 2):
            got["gy", n, k].wait_recv()
        for k in (2, 1, 3):
            piece = gg.at[pl.ds(own_x, 64), spans[n]]
            got["gx", n, k] = copy(piece, piece, device(dx=k))

    def arrived(n):
        for k in (1, 3, 2):
            got["gx", n, k].wait_recv()

    gram(0)
    forward(0)
    forward(1)
    gram(1)
    sum_x(0)
    for which in (0, 1):
        got[which, 3].wait_recv()
    gram(2)
    sum_x(1)
    for which in (0, 1):
        got[which, 4].wait_recv()
    gram(3)
    sum_y(0)
    sum_y(1)
    sum_x(2)
    gather_x(0)
    sum_x(3)
    gather_x(1)
    sum_y(2)
    sum_y(3)
    gather_x(2)
    gather_x(3)
    for n in range(len(CHUNKS)):
        arrived(n)

    half[...] = jnp.zeros_like(half)
    for chunk in CHUNKS:
        for i, j, w in chunk:
            if w == 128:
                rows, columns, begin = halved(i, j)
                gap = gg[:, columns_of[i, j]]
                half[rows - 2] += dot(gap, sb[columns - 1, pl.ds(begin, 128)], ((1,), (0,)))
                half[columns - 2, pl.ds(begin, 128)] += dot(gap, sb[rows - 1], ((0,), (0,)))

    def gradient(k):
        total = half[k - 2] if k >= 2 else None
        for chunk in CHUNKS:
            for i, j, w in chunk:
                if w == 256 and k in (i, j):
                    gap = gg[:, columns_of[i, j]]
                    if k == i:
                        term = dot(gap, slot(0, j)[...], ((1,), (0,)))
                    else:
                        term = dot(gap, slot(0, i)[...], ((0,), (0,)))
                    total = term if total is None else total + term
        return total

    for k in (3, 4, 2, 1):
        ps[k - 1] = gradient(k).astype(BF16)
        got["f", k] = copy(ps.at[k - 1], fr.at[k - 1], device(dl=COVER[k][0], dz=COVER[k][1]))
    total = gradient(0)
    for k in (1, 2, 4, 3):
        got["f", k].wait_recv()
        total += fr[k - 1].astype(F32)
    out_ref[0] = total.astype(BF16)
    for made in started:
        made.wait_send()


def body(student, teacher):
    scale = 1.0 / (student.shape[2] * lax.axis_size("row"))
    blocks = pltpu.VMEM((4, 256, 256), BF16)
    return pl.pallas_call(
        functools.partial(kernel, scale),
        out_shape=jax.ShapeDtypeStruct(student.shape, BF16),
        in_specs=[pl.BlockSpec(memory_space=pltpu.VMEM)] * 2,
        out_specs=pl.BlockSpec(memory_space=pltpu.VMEM),
        scratch_shapes=[
            blocks,
            blocks,
            pltpu.VMEM((256, WIDTH), BF16),
            pltpu.VMEM((256, WIDTH), F32),
            pltpu.VMEM((3, 64, WIDTH), BF16),
            pltpu.VMEM((64, WIDTH), BF16),
            pltpu.VMEM((64, WIDTH), F32),
            pltpu.VMEM((3, 16, WIDTH), BF16),
            pltpu.VMEM((256, WIDTH), BF16),
            pltpu.VMEM((3, 256, 256), F32),
            blocks,
            blocks,
            pltpu.SemaphoreType.DMA((COPIES,)),
            pltpu.SemaphoreType.DMA((COPIES,)),
        ],
        compiler_params=pltpu.CompilerParams(
            collective_id=0, has_side_effects=True, vmem_limit_bytes=32 * 1024 * 1024
        ),
    )(student, teacher)


def solution(mesh):
    placed = P("img", "col", "row")
    return jax.shard_map(
        body, mesh=mesh, in_specs=(placed, placed), out_specs=placed, check_vma=False
    )
```

```python
import functools

import jax
import jax.numpy as jnp
from jax import lax
from jax.experimental import pallas as pl
from jax.experimental.pallas import tpu as pltpu
from jax.sharding import PartitionSpec as P

MESH = pl.DeviceIdType.MESH
F32, BF16 = jnp.float32, jnp.bfloat16

COVER = ((0, 0), (0, 1), (0, 3), (0, -1), (1, 0), (1, -1))
CHUNKS = (
    ((0, 0, 256),),
    ((0, 1, 256),),
    ((1, 3, 256), (1, 4, 256), (0, 4, 128)),
    ((1, 5, 256),),
    ((0, 2, 256), (2, 3, 128)),
    ((2, 4, 256), (2, 5, 128)),
)
WHOLE = (3, 4, 5)
WIDTH = sum(w for chunk in CHUNKS for _, _, w in chunk)
HELD = len(COVER)
COPIES = 3 * (HELD - 1) + 12 * len(CHUNKS) - 3 * len(WHOLE)


def dot(a, b, dims):
    return lax.dot_general(a, b, (dims, ((), ())), preferred_element_type=F32)


def kernel(scale, s_ref, t_ref, out_ref, sb, tb, gs, gf, rx, xs, xf, ry, gg, half, ps, fr, send, recv, local):
    r, c, img = lax.axis_index("row"), lax.axis_index("col"), lax.axis_index("img")
    x, h, l, z = r // 4, r % 4, c // 8, c % 8
    way = 1 - 2 * img

    def device(dx=0, dh=0, dl=0, dz=0):
        return (
            (x + dx) % 4 * 4 + (h + dh) % 4,
            (l + dl) % 2 * 8 + (z + 8 + way * dz) % 8,
            img,
        )

    count = [0]
    pending = []

    def copy(src, dst, to):
        k = count[0]
        count[0] += 1
        made = pltpu.make_async_remote_copy(
            src_ref=src, dst_ref=dst, send_sem=send.at[k], recv_sem=recv.at[k],
            device_id=to, device_id_type=MESH,
        )
        made.start()
        pending.append(made)
        return made

    def sent(made):
        pending.remove(made)
        made.wait_send()

    own_copies = [
        pltpu.make_async_copy(ref.at[0], held.at[0], local.at[k])
        for k, (ref, held) in enumerate(((s_ref, sb), (t_ref, tb)))
    ]
    for made in own_copies:
        made.start()

    peers = [device(dl=a, dz=b) for a, b in ((0, 1), (0, -1), (1, 0), (0, 2), (0, -3), (1, 1))]
    peers += [device(dx=k) for k in (1, 2, 3)] + [device(dh=k) for k in (1, 2, 3)]
    barrier = pltpu.get_barrier_semaphore()
    for peer in peers:
        pl.semaphore_signal(barrier, inc=1, device_id=peer, device_id_type=MESH)
    pl.semaphore_wait(barrier, len(peers))

    held = (sb, tb)
    got = {}

    def first(which, k, to):
        own = (s_ref, t_ref)[which].at[0]
        got[which, k] = copy(own, held[which].at[k], to)

    def forward(which, k, to_slot, to):
        got[which, k].wait_recv()
        got[which, to_slot] = copy(held[which].at[k], held[which].at[to_slot], to)

    def halved(i, j):
        first = (z < 4) if COVER[i][0] == COVER[j][0] else (l == 0)
        f = jnp.where(first, 1, 0)
        rows, columns = i * f + j * (1 - f), j * f + i * (1 - f)
        return rows, columns, pl.multiple_of((1 - f) * 128, 128)

    columns_of = {}
    spans = []
    at = 0
    for chunk in CHUNKS:
        begin = at
        for i, j, w in chunk:
            columns_of[i, j] = pl.ds(at, w)
            at += w
        spans.append(pl.ds(begin, at - begin))

    def gram(n):
        for i, j, w in CHUNKS[n]:
            if w == 256:
                a_s, b_s, a_t, b_t = sb[i], sb[j], tb[i], tb[j]
            else:
                rows, columns, begin = halved(i, j)
                a_s, a_t = sb[rows], tb[rows]
                b_s, b_t = sb[columns, pl.ds(begin, 128)], tb[columns, pl.ds(begin, 128)]
            part = (dot(a_s, b_s, ((1,), (1,))) - dot(a_t, b_t, ((1,), (1,)))) * scale
            gf[:, columns_of[i, j]] = part
            gs[:, columns_of[i, j]] = part.astype(BF16)
        for k in (2, 1, 3):
            rows = pl.multiple_of((x + k) % 4 * 64, 64)
            got["sx", n, k] = copy(gs.at[pl.ds(rows, 64), spans[n]], rx.at[k - 1, :, spans[n]], device(dx=k))

    own_x = pl.multiple_of(x * 64, 64)
    own_y = pl.multiple_of(h * 16, 16)
    own = pl.multiple_of(x * 64 + h * 16, 16)

    def sum_x(n):
        for k in (1, 3, 2):
            got["sx", n, k].wait_recv()
        total = gf[pl.ds(own_x, 64), spans[n]]
        for k in range(3):
            total += rx[k, :, spans[n]].astype(F32)
        xf[:, spans[n]] = total
        xs[:, spans[n]] = total.astype(BF16)
        for k in (2, 1, 3):
            if n in WHOLE:
                got["sy", n, k] = copy(xs.at[:, spans[n]], ry.at[k - 1, :, spans[n]], device(dh=k))
            else:
                rows = pl.multiple_of((h + k) % 4 * 16, 16)
                to = ry.at[k - 1, pl.ds(0, 16), spans[n]]
                got["sy", n, k] = copy(xs.at[pl.ds(rows, 16), spans[n]], to, device(dh=k))

    def sum_y(n):
        for k in (1, 3, 2):
            got["sy", n, k].wait_recv()
        if n in WHOLE:
            total = xf[:, spans[n]]
            for k in range(3):
                total += ry[k, :, spans[n]].astype(F32)
            gg[pl.ds(own_x, 64), spans[n]] = total.astype(BF16)
            return
        total = xf[pl.ds(own_y, 16), spans[n]]
        for k in range(3):
            total += ry[k, pl.ds(0, 16), spans[n]].astype(F32)
        gg[pl.ds(own, 16), spans[n]] = total.astype(BF16)
        for k in (2, 1, 3):
            piece = gg.at[pl.ds(own, 16), spans[n]]
            got["gy", n, k] = copy(piece, piece, device(dh=k))

    def gather_x(n):
        if n not in WHOLE:
            for k in (1, 3, 2):
                got["gy", n, k].wait_recv()
        for k in (2, 1, 3):
            piece = gg.at[pl.ds(own_x, 64), spans[n]]
            got["gx", n, k] = copy(piece, piece, device(dx=k))

    def arrived(n):
        for k in (1, 3, 2):
            got["gx", n, k].wait_recv()

    for k, to in ((1, device(dz=-1)), (4, device(dl=1))):
        for which in (0, 1):
            first(which, k, to)
    for made in own_copies:
        made.wait()
    gram(0)
    for which in (0, 1):
        first(which, 3, device(dz=1))
    for which in (0, 1):
        forward(which, 1, 2, device(dz=-2))
    gram(1)
    sum_x(0)
    for which in (0, 1):
        forward(which, 3, 5, device(dl=1))
    for which in (0, 1):
        got[which, 4].wait_recv()
    gram(2)
    sum_x(1)
    sum_y(0)
    for which in (0, 1):
        got[which, 5].wait_recv()
    gram(3)
    for which in (0, 1):
        got[which, 2].wait_recv()
    gram(4)
    gram(5)
    sum_x(2)
    sum_y(1)
    gather_x(0)
    sum_x(3)
    gather_x(1)
    sum_y(2)
    sum_x(4)
    sum_x(5)
    gather_x(2)
    sum_y(3)
    gather_x(3)
    sum_y(4)
    gather_x(4)
    sum_y(5)
    gather_x(5)
    for n in range(4):
        arrived(n)

    def halves(n):
        for i, j, w in CHUNKS[n]:
            if w == 128:
                rows, columns, begin = halved(i, j)
                gap = gg[:, columns_of[i, j]]
                half[rows] += dot(gap, sb[columns, pl.ds(begin, 128)], ((1,), (0,)))
                half[columns, pl.ds(begin, 128)] += dot(gap, sb[rows], ((0,), (0,)))

    def gradient(k):
        total = half[k] if k != 1 else None
        for chunk in CHUNKS:
            for i, j, w in chunk:
                if w == 256 and k in (i, j):
                    gap = gg[:, columns_of[i, j]]
                    if k == i:
                        term = dot(gap, sb[j], ((1,), (0,)))
                    else:
                        term = dot(gap, sb[i], ((0,), (0,)))
                    total = term if total is None else total + term
        return total

    def give(k):
        ps[k - 1] = gradient(k).astype(BF16)
        got["f", k] = copy(ps.at[k - 1], fr.at[k - 1], device(dl=COVER[k][0], dz=COVER[k][1]))

    half[...] = jnp.zeros_like(half)
    halves(2)
    give(1)
    arrived(4)
    halves(4)
    give(3)
    arrived(5)
    halves(5)
    for k in (2, 5, 4):
        give(k)
    total = gradient(0)
    for k in (1, 3, 4, 5, 2):
        got["f", k].wait_recv()
        total += fr[k - 1].astype(F32)
    out_ref[0] = total.astype(BF16)
    for made in pending:
        made.wait_send()


def body(student, teacher):
    scale = 1.0 / (student.shape[2] * lax.axis_size("row"))
    blocks = pltpu.VMEM((HELD, 256, 256), BF16)
    partials = pltpu.VMEM((HELD - 1, 256, 256), BF16)
    return pl.pallas_call(
        functools.partial(kernel, scale),
        out_shape=jax.ShapeDtypeStruct(student.shape, BF16),
        in_specs=[pl.BlockSpec(memory_space=pl.ANY)] * 2,
        out_specs=pl.BlockSpec(memory_space=pltpu.VMEM),
        scratch_shapes=[
            blocks,
            blocks,
            pltpu.VMEM((256, WIDTH), BF16),
            pltpu.VMEM((256, WIDTH), F32),
            pltpu.VMEM((3, 64, WIDTH), BF16),
            pltpu.VMEM((64, WIDTH), BF16),
            pltpu.VMEM((64, WIDTH), F32),
            pltpu.VMEM((3, 64, WIDTH), BF16),
            pltpu.VMEM((256, WIDTH), BF16),
            pltpu.VMEM((HELD, 256, 256), F32),
            partials,
            partials,
            pltpu.SemaphoreType.DMA((COPIES,)),
            pltpu.SemaphoreType.DMA((COPIES,)),
            pltpu.SemaphoreType.DMA((2,)),
        ],
        compiler_params=pltpu.CompilerParams(
            collective_id=0, has_side_effects=True, vmem_limit_bytes=55040 * 1024
        ),
    )(student, teacher)


def solution(mesh):
    placed = P("img", "col", "row")
    return jax.shard_map(
        body, mesh=mesh, in_specs=(placed, placed), out_specs=placed, check_vma=False
    )
```

```python
import functools

import jax
import jax.numpy as jnp
from jax import lax
from jax.experimental import pallas as pl
from jax.experimental.pallas import tpu as pltpu
from jax.sharding import PartitionSpec as P

MESH = pl.DeviceIdType.MESH
F32, BF16 = jnp.float32, jnp.bfloat16

COVER = ((0, 0), (0, 1), (0, 3), (0, -1), (1, 0), (1, -1))
CHUNKS = (
    ((0, 0, 256),),
    ((0, 1, 256),),
    ((1, 3, 256), (1, 4, 256), (0, 4, 128)),
    ((1, 5, 256),),
    ((0, 2, 256), (2, 3, 128)),
    ((2, 4, 256), (2, 5, 128)),
)
WHOLE = (3, 4, 5)
WIDTHS = [sum(w for _, _, w in chunk) for chunk in CHUNKS]
HELD = len(COVER)
COPIES = 3 * (HELD - 1) + 12 * len(CHUNKS) - 3 * len(WHOLE)


def dot(a, b, dims):
    return lax.dot_general(a, b, (dims, ((), ())), preferred_element_type=F32)


def kernel(scale, s_ref, t_ref, out_ref, sb, tb, gs, gf, rx, xs, xf, ry, gg, half, ps, fr, send, recv, local):
    r, c, img = lax.axis_index("row"), lax.axis_index("col"), lax.axis_index("img")
    x, h, l, z = r // 4, r % 4, c // 8, c % 8
    way = 1 - 2 * img

    def device(dx=0, dh=0, dl=0, dz=0):
        return (
            (x + dx) % 4 * 4 + (h + dh) % 4,
            (l + dl) % 2 * 8 + (z + 8 + way * dz) % 8,
            img,
        )

    count = [0]
    pending = []

    def copy(src, dst, to):
        k = count[0]
        count[0] += 1
        made = pltpu.make_async_remote_copy(
            src_ref=src, dst_ref=dst, send_sem=send.at[k], recv_sem=recv.at[k],
            device_id=to, device_id_type=MESH,
        )
        made.start()
        pending.append(made)
        return made

    def sent(made):
        pending.remove(made)
        made.wait_send()

    own_copies = [
        pltpu.make_async_copy(ref.at[0], held.at[0], local.at[k])
        for k, (ref, held) in enumerate(((s_ref, sb), (t_ref, tb)))
    ]
    for made in own_copies:
        made.start()

    peers = [device(dl=a, dz=b) for a, b in ((0, 1), (0, -1), (1, 0), (0, 2))]
    peers += [device(dx=k) for k in (1, 2, 3)] + [device(dh=k) for k in (1, 2, 3)]
    barrier = pltpu.get_barrier_semaphore()
    for peer in peers:
        pl.semaphore_signal(barrier, inc=1, device_id=peer, device_id_type=MESH)
    pl.semaphore_wait(barrier, len(peers))

    held = (sb, tb)
    got = {}

    def first(which, k, to):
        own = (s_ref, t_ref)[which].at[0]
        got[which, k] = copy(own, held[which].at[k], to)

    def forward(which, k, to_slot, to):
        got[which, k].wait_recv()
        got[which, to_slot] = copy(held[which].at[k], held[which].at[to_slot], to)

    def halved(i, j):
        first = (z < 4) if COVER[i][0] == COVER[j][0] else (l == 0)
        f = jnp.where(first, 1, 0)
        rows, columns = i * f + j * (1 - f), j * f + i * (1 - f)
        return rows, columns, pl.multiple_of((1 - f) * 128, 128)

    place = {}
    for n, chunk in enumerate(CHUNKS):
        at = 0
        for i, j, w in chunk:
            place[i, j] = n, pl.ds(at, w)
            at += w

    def gram(n):
        for i, j, w in CHUNKS[n]:
            if w == 256:
                a_s, b_s, a_t, b_t = sb[i], sb[j], tb[i], tb[j]
            else:
                rows, columns, begin = halved(i, j)
                a_s, a_t = sb[rows], tb[rows]
                b_s, b_t = sb[columns, pl.ds(begin, 128)], tb[columns, pl.ds(begin, 128)]
            part = (dot(a_s, b_s, ((1,), (1,))) - dot(a_t, b_t, ((1,), (1,)))) * scale
            gf[n][:, place[i, j][1]] = part
            gs[n][:, place[i, j][1]] = part.astype(BF16)
        for k in (2, 1, 3):
            rows = pl.multiple_of((x + k) % 4 * 64, 64)
            got["sx", n, k] = copy(gs[n].at[pl.ds(rows, 64)], rx[n].at[k - 1], device(dx=k))

    own_x = pl.multiple_of(x * 64, 64)
    own_y = pl.multiple_of(h * 16, 16)
    own = pl.multiple_of(x * 64 + h * 16, 16)

    def sum_x(n):
        for k in (1, 3, 2):
            got["sx", n, k].wait_recv()
        total = gf[n][pl.ds(own_x, 64)]
        for k in range(3):
            total += rx[n][k].astype(F32)
        xf[n][...] = total
        xs[n][...] = total.astype(BF16)
        for k in (2, 1, 3):
            if n in WHOLE:
                got["sy", n, k] = copy(xs[n], ry[n].at[k - 1], device(dh=k))
            else:
                rows = pl.multiple_of((h + k) % 4 * 16, 16)
                to = ry[n].at[k - 1, pl.ds(0, 16)]
                got["sy", n, k] = copy(xs[n].at[pl.ds(rows, 16)], to, device(dh=k))

    def sum_y(n):
        for k in (1, 3, 2):
            got["sy", n, k].wait_recv()
        if n in WHOLE:
            total = xf[n][...]
            for k in range(3):
                total += ry[n][k].astype(F32)
            gg[n][pl.ds(own_x, 64)] = total.astype(BF16)
            return
        total = xf[n][pl.ds(own_y, 16)]
        for k in range(3):
            total += ry[n][k, pl.ds(0, 16)].astype(F32)
        gg[n][pl.ds(own, 16)] = total.astype(BF16)
        for k in (2, 1, 3):
            piece = gg[n].at[pl.ds(own, 16)]
            got["gy", n, k] = copy(piece, piece, device(dh=k))

    def gather_x(n):
        if n not in WHOLE:
            for k in (1, 3, 2):
                got["gy", n, k].wait_recv()
        for k in (2, 1, 3):
            piece = gg[n].at[pl.ds(own_x, 64)]
            got["gx", n, k] = copy(piece, piece, device(dx=k))

    def arrived(n):
        for k in (1, 3, 2):
            got["gx", n, k].wait_recv()

    for k, to in ((1, device(dz=-1)), (4, device(dl=1))):
        for which in (0, 1):
            first(which, k, to)
    for made in own_copies:
        made.wait()
    gram(0)
    for which in (0, 1):
        first(which, 3, device(dz=1))
    for which in (0, 1):
        forward(which, 1, 2, device(dz=-2))
    gram(1)
    sum_x(0)
    for which in (0, 1):
        forward(which, 3, 5, device(dl=1))
    for which in (0, 1):
        got[which, 4].wait_recv()
    gram(2)
    sum_x(1)
    sum_y(0)
    for which in (0, 1):
        got[which, 5].wait_recv()
    gram(3)
    for which in (0, 1):
        got[which, 2].wait_recv()
    gram(4)
    gram(5)
    half[...] = jnp.zeros_like(half)
    sum_x(2)
    sum_y(1)
    gather_x(0)
    sum_x(3)
    gather_x(1)
    sum_y(2)
    sum_x(4)
    sum_x(5)
    sum_y(3)
    gather_x(3)
    gather_x(2)
    sum_y(4)
    gather_x(4)
    sum_y(5)
    gather_x(5)
    for n in range(4):
        arrived(n)

    def halves(n):
        for i, j, w in CHUNKS[n]:
            if w == 128:
                rows, columns, begin = halved(i, j)
                gap = gg[place[i, j][0]][:, place[i, j][1]]
                half[rows] += dot(gap, sb[columns, pl.ds(begin, 128)], ((1,), (0,)))
                half[columns, pl.ds(begin, 128)] += dot(gap, sb[rows], ((0,), (0,)))

    def gradient(k, chunks):
        total = half[k]
        for n in chunks:
            for i, j, w in CHUNKS[n]:
                if w == 256 and k in (i, j):
                    gap = gg[n][:, place[i, j][1]]
                    if k == i:
                        total = total + dot(gap, sb[j], ((1,), (0,)))
                    else:
                        total = total + dot(gap, sb[i], ((0,), (0,)))
        return total

    def give(k, chunks):
        ps[k - 1] = gradient(k, chunks).astype(BF16)
        got["f", k] = copy(ps.at[k - 1], fr.at[k - 1], device(dl=COVER[k][0], dz=COVER[k][1]))

    halves(2)
    give(1, range(4))
    arrived(4)
    halves(4)
    give(3, range(5))
    for k in (2, 5, 4, 0):
        half[k] = gradient(k, range(5))
    arrived(5)
    halves(5)
    for k in (2, 5, 4):
        give(k, (5,))
    total = half[0]
    for k in (1, 3, 4, 5, 2):
        got["f", k].wait_recv()
        total += fr[k - 1].astype(F32)
    out_ref[0] = total.astype(BF16)
    for made in pending:
        made.wait_send()


def by_chunk(shape, dtype):
    return tuple(pltpu.VMEM((*shape, w), dtype) for w in WIDTHS)


def body(student, teacher):
    scale = 1.0 / (student.shape[2] * lax.axis_size("row"))
    blocks = pltpu.VMEM((HELD, 256, 256), BF16)
    partials = pltpu.VMEM((HELD - 1, 256, 256), BF16)
    return pl.pallas_call(
        functools.partial(kernel, scale),
        out_shape=jax.ShapeDtypeStruct(student.shape, BF16),
        in_specs=[pl.BlockSpec(memory_space=pl.ANY)] * 2,
        out_specs=pl.BlockSpec(memory_space=pltpu.VMEM),
        scratch_shapes=[
            blocks,
            blocks,
            by_chunk((256,), BF16),
            by_chunk((256,), F32),
            by_chunk((3, 64), BF16),
            by_chunk((64,), BF16),
            by_chunk((64,), F32),
            by_chunk((3, 64), BF16),
            by_chunk((256,), BF16),
            pltpu.VMEM((HELD, 256, 256), F32),
            partials,
            partials,
            pltpu.SemaphoreType.DMA((COPIES,)),
            pltpu.SemaphoreType.DMA((COPIES,)),
            pltpu.SemaphoreType.DMA((2,)),
        ],
        compiler_params=pltpu.CompilerParams(
            collective_id=0, has_side_effects=True, vmem_limit_bytes=55040 * 1024
        ),
    )(student, teacher)


def solution(mesh):
    placed = P("img", "col", "row")
    return jax.shard_map(
        body, mesh=mesh, in_specs=(placed, placed), out_specs=placed, check_vma=False
    )
```

```python
import functools

import jax
import jax.numpy as jnp
from jax import lax
from jax.experimental import pallas as pl
from jax.experimental.pallas import tpu as pltpu
from jax.sharding import PartitionSpec as P

MESH = pl.DeviceIdType.MESH
F32, BF16 = jnp.float32, jnp.bfloat16

COVER = ((0, 0), (0, 1), (0, 3), (0, -1), (1, 0), (1, -1))
CHUNKS = (
    ((0, 0, 256),),
    ((0, 1, 256),),
    ((1, 3, 256), (1, 4, 256), (0, 4, 128)),
    ((1, 5, 256),),
    ((0, 2, 256), (2, 3, 128)),
    ((2, 4, 256), (2, 5, 128)),
)
WHOLE = (3, 4, 5)
WIDTHS = [sum(w for _, _, w in chunk) for chunk in CHUNKS]
HELD = len(COVER)
COPIES = 3 * (HELD - 1) + 12 * len(CHUNKS) - 3 * len(WHOLE)


def dot(a, b, dims):
    return lax.dot_general(a, b, (dims, ((), ())), preferred_element_type=F32)


def kernel(scale, s_ref, t_ref, out_ref, sb, tb, gs, gf, rx, xs, xf, ry, gg, half, ps, fr, send, recv, local):
    r, c, img = lax.axis_index("row"), lax.axis_index("col"), lax.axis_index("img")
    x, h, l, z = r // 4, r % 4, c // 8, c % 8
    way = 1 - 2 * img

    def device(dx=0, dh=0, dl=0, dz=0):
        return (
            (x + dx) % 4 * 4 + (h + dh) % 4,
            (l + dl) % 2 * 8 + (z + 8 + way * dz) % 8,
            img,
        )

    count = [0]
    pending = []

    def copy(src, dst, to):
        k = count[0]
        count[0] += 1
        made = pltpu.make_async_remote_copy(
            src_ref=src, dst_ref=dst, send_sem=send.at[k], recv_sem=recv.at[k],
            device_id=to, device_id_type=MESH,
        )
        made.start()
        pending.append(made)
        return made

    def sent(made):
        pending.remove(made)
        made.wait_send()

    own_copies = [
        pltpu.make_async_copy(ref.at[0], held.at[0], local.at[k])
        for k, (ref, held) in enumerate(((s_ref, sb), (t_ref, tb)))
    ]
    for made in own_copies:
        made.start()

    peers = [device(dl=a, dz=b) for a, b in ((0, 1), (0, -1), (1, 0), (0, 2))]
    peers += [device(dx=k) for k in (1, 2, 3)] + [device(dh=k) for k in (1, 2, 3)]
    barrier = pltpu.get_barrier_semaphore()
    for peer in peers:
        pl.semaphore_signal(barrier, inc=1, device_id=peer, device_id_type=MESH)
    pl.semaphore_wait(barrier, len(peers))

    held = (sb, tb)
    got = {}

    def first(which, k, to):
        own = (s_ref, t_ref)[which].at[0]
        got[which, k] = copy(own, held[which].at[k], to)

    def forward(which, k, to_slot, to):
        got[which, k].wait_recv()
        got[which, to_slot] = copy(held[which].at[k], held[which].at[to_slot], to)

    def halved(i, j):
        first = (z < 4) if COVER[i][0] == COVER[j][0] else (l == 0)
        f = jnp.where(first, 1, 0)
        rows, columns = i * f + j * (1 - f), j * f + i * (1 - f)
        return rows, columns, pl.multiple_of((1 - f) * 128, 128)

    place = {}
    for n, chunk in enumerate(CHUNKS):
        at = 0
        for i, j, w in chunk:
            place[i, j] = n, pl.ds(at, w)
            at += w

    def gram(n):
        for i, j, w in CHUNKS[n]:
            if w == 256:
                a_s, b_s, a_t, b_t = sb[i], sb[j], tb[i], tb[j]
            else:
                rows, columns, begin = halved(i, j)
                a_s, a_t = sb[rows], tb[rows]
                b_s, b_t = sb[columns, pl.ds(begin, 128)], tb[columns, pl.ds(begin, 128)]
            part = (dot(a_s, b_s, ((1,), (1,))) - dot(a_t, b_t, ((1,), (1,)))) * scale
            gf[n][:, place[i, j][1]] = part
            gs[n][:, place[i, j][1]] = part.astype(BF16)
        for k in (2, 1, 3):
            rows = pl.multiple_of((x + k) % 4 * 64, 64)
            got["sx", n, k] = copy(gs[n].at[pl.ds(rows, 64)], rx[n].at[k - 1], device(dx=k))

    own_x = pl.multiple_of(x * 64, 64)
    own_y = pl.multiple_of(h * 16, 16)
    own = pl.multiple_of(x * 64 + h * 16, 16)

    def sum_x(n):
        for k in (1, 3, 2):
            got["sx", n, k].wait_recv()
        total = gf[n][pl.ds(own_x, 64)]
        for k in range(3):
            total += rx[n][k].astype(F32)
        xf[n][...] = total
        xs[n][...] = total.astype(BF16)
        for k in (2, 1, 3):
            if n in WHOLE:
                got["sy", n, k] = copy(xs[n], ry[n].at[k - 1], device(dh=k))
            else:
                rows = pl.multiple_of((h + k) % 4 * 16, 16)
                to = ry[n].at[k - 1, pl.ds(0, 16)]
                got["sy", n, k] = copy(xs[n].at[pl.ds(rows, 16)], to, device(dh=k))

    def sum_y(n):
        for k in (1, 3, 2):
            got["sy", n, k].wait_recv()
        if n in WHOLE:
            total = xf[n][...]
            for k in range(3):
                total += ry[n][k].astype(F32)
            gg[n][pl.ds(own_x, 64)] = total.astype(BF16)
            return
        total = xf[n][pl.ds(own_y, 16)]
        for k in range(3):
            total += ry[n][k, pl.ds(0, 16)].astype(F32)
        gg[n][pl.ds(own, 16)] = total.astype(BF16)
        for k in (2, 1, 3):
            piece = gg[n].at[pl.ds(own, 16)]
            got["gy", n, k] = copy(piece, piece, device(dh=k))

    def gather_x(n):
        if n not in WHOLE:
            for k in (1, 3, 2):
                got["gy", n, k].wait_recv()
        for k in (2, 1, 3):
            piece = gg[n].at[pl.ds(own_x, 64)]
            got["gx", n, k] = copy(piece, piece, device(dx=k))

    def arrived(n):
        for k in (1, 3, 2):
            got["gx", n, k].wait_recv()

    for k, to in ((1, device(dz=-1)), (4, device(dl=1))):
        for which in (0, 1):
            first(which, k, to)
    for made in own_copies:
        made.wait()
    gram(0)
    for which in (0, 1):
        first(which, 3, device(dz=1))
    for which in (0, 1):
        forward(which, 1, 2, device(dz=-2))
    gram(1)
    sum_x(0)
    for which in (0, 1):
        forward(which, 3, 5, device(dl=1))
    for which in (0, 1):
        got[which, 4].wait_recv()
    gram(2)
    sum_x(1)
    sum_y(0)
    for which in (0, 1):
        got[which, 5].wait_recv()
    for which in (0, 1):
        got[which, 2].wait_recv()
    gram(4)
    gram(5)
    gram(3)
    half[...] = jnp.zeros_like(half)
    sum_x(2)
    sum_y(1)
    gather_x(0)
    sum_x(4)
    gather_x(1)
    sum_y(2)
    sum_x(5)
    sum_x(3)
    sum_y(4)
    gather_x(4)
    gather_x(2)
    sum_y(5)
    gather_x(5)
    sum_y(3)
    gather_x(3)
    for n in (0, 1, 2, 4):
        arrived(n)

    def halves(n):
        for i, j, w in CHUNKS[n]:
            if w == 128:
                rows, columns, begin = halved(i, j)
                gap = gg[place[i, j][0]][:, place[i, j][1]]
                half[rows] += dot(gap, sb[columns, pl.ds(begin, 128)], ((1,), (0,)))
                half[columns, pl.ds(begin, 128)] += dot(gap, sb[rows], ((0,), (0,)))

    def gradient(k, chunks):
        total = half[k]
        for n in chunks:
            for i, j, w in CHUNKS[n]:
                if w == 256 and k in (i, j):
                    gap = gg[n][:, place[i, j][1]]
                    if k == i:
                        total = total + dot(gap, sb[j], ((1,), (0,)))
                    else:
                        total = total + dot(gap, sb[i], ((0,), (0,)))
        return total

    def give(k, chunks):
        ps[k - 1] = gradient(k, chunks).astype(BF16)
        got["f", k] = copy(ps.at[k - 1], fr.at[k - 1], device(dl=COVER[k][0], dz=COVER[k][1]))

    halves(2)
    halves(4)
    give(3, (2,))
    for k in (2, 4):
        half[k] = gradient(k, (2, 4))
    arrived(5)
    halves(5)
    give(2, (5,))
    give(4, (5,))
    half[0] = gradient(0, (0, 1, 2, 4))
    half[1] = gradient(1, (1, 2))
    arrived(3)
    give(5, (3,))
    give(1, (3,))
    total = half[0]
    for k in (3, 4, 2, 1, 5):
        got["f", k].wait_recv()
        total += fr[k - 1].astype(F32)
    out_ref[0] = total.astype(BF16)
    for made in pending:
        made.wait_send()


def by_chunk(shape, dtype):
    return tuple(pltpu.VMEM((*shape, w), dtype) for w in WIDTHS)


def body(student, teacher):
    scale = 1.0 / (student.shape[2] * lax.axis_size("row"))
    blocks = pltpu.VMEM((HELD, 256, 256), BF16)
    partials = pltpu.VMEM((HELD - 1, 256, 256), BF16)
    return pl.pallas_call(
        functools.partial(kernel, scale),
        out_shape=jax.ShapeDtypeStruct(student.shape, BF16),
        in_specs=[pl.BlockSpec(memory_space=pl.ANY)] * 2,
        out_specs=pl.BlockSpec(memory_space=pltpu.VMEM),
        scratch_shapes=[
            blocks,
            blocks,
            by_chunk((256,), BF16),
            by_chunk((256,), F32),
            by_chunk((3, 64), BF16),
            by_chunk((64,), BF16),
            by_chunk((64,), F32),
            by_chunk((3, 64), BF16),
            by_chunk((256,), BF16),
            pltpu.VMEM((HELD, 256, 256), F32),
            partials,
            partials,
            pltpu.SemaphoreType.DMA((COPIES,)),
            pltpu.SemaphoreType.DMA((COPIES,)),
            pltpu.SemaphoreType.DMA((2,)),
        ],
        compiler_params=pltpu.CompilerParams(
            collective_id=0, has_side_effects=True, vmem_limit_bytes=55040 * 1024
        ),
    )(student, teacher)


def solution(mesh):
    placed = P("img", "col", "row")
    return jax.shard_map(
        body, mesh=mesh, in_specs=(placed, placed), out_specs=placed, check_vma=False
    )
```

```python
import functools

import jax
import jax.numpy as jnp
from jax import lax
from jax.experimental import pallas as pl
from jax.experimental.pallas import tpu as pltpu
from jax.sharding import PartitionSpec as P

MESH = pl.DeviceIdType.MESH
F32, BF16 = jnp.float32, jnp.bfloat16

COVER = ((0, 0), (0, 1), (0, 3), (0, -1), (1, 0), (1, -1))
CHUNKS = (
    ((0, 0, 256),),
    ((0, 1, 256),),
    ((1, 3, 256), (1, 4, 256), (0, 4, 128)),
    ((1, 5, 256),),
    ((0, 2, 256), (2, 3, 128)),
    ((2, 4, 256), (2, 5, 128)),
)
WHOLE = (3, 4, 5)
WIDTHS = [sum(w for _, _, w in chunk) for chunk in CHUNKS]
HELD = len(COVER)
COPIES = 3 * (HELD - 1) + 12 * len(CHUNKS) - 3 * len(WHOLE)


def dot(a, b, dims):
    return lax.dot_general(a, b, (dims, ((), ())), preferred_element_type=F32)


def kernel(scale, s_ref, t_ref, out_ref, sb, tb, gs, gf, rx, xs, xf, ry, gg, half, ps, fr, send, recv, local):
    r, c, img = lax.axis_index("row"), lax.axis_index("col"), lax.axis_index("img")
    x, h, l, z = r // 4, r % 4, c // 8, c % 8
    way = 1 - 2 * img

    def device(dx=0, dh=0, dl=0, dz=0):
        return (
            (x + dx) % 4 * 4 + (h + dh) % 4,
            (l + dl) % 2 * 8 + (z + 8 + way * dz) % 8,
            img,
        )

    count = [0]
    pending = []

    def copy(src, dst, to):
        k = count[0]
        count[0] += 1
        made = pltpu.make_async_remote_copy(
            src_ref=src, dst_ref=dst, send_sem=send.at[k], recv_sem=recv.at[k],
            device_id=to, device_id_type=MESH,
        )
        made.start()
        pending.append(made)
        return made

    def sent(made):
        pending.remove(made)
        made.wait_send()

    own_copies = [
        pltpu.make_async_copy(ref.at[0], held.at[0], local.at[k])
        for k, (ref, held) in enumerate(((s_ref, sb), (t_ref, tb)))
    ]
    for made in own_copies:
        made.start()

    peers = [device(dl=a, dz=b) for a, b in ((0, 1), (0, -1), (1, 0), (0, 2))]
    peers += [device(dx=k) for k in (1, 2, 3)] + [device(dh=k) for k in (1, 2, 3)]
    barrier = pltpu.get_barrier_semaphore()
    for peer in peers:
        pl.semaphore_signal(barrier, inc=1, device_id=peer, device_id_type=MESH)
    pl.semaphore_wait(barrier, len(peers))

    held = (sb, tb)
    got = {}

    def first(which, k, to):
        own = (s_ref, t_ref)[which].at[0]
        got[which, k] = copy(own, held[which].at[k], to)

    def forward(which, k, to_slot, to):
        got[which, k].wait_recv()
        got[which, to_slot] = copy(held[which].at[k], held[which].at[to_slot], to)

    def halved(i, j):
        first = (z < 4) if COVER[i][0] == COVER[j][0] else (l == 0)
        f = jnp.where(first, 1, 0)
        rows, columns = i * f + j * (1 - f), j * f + i * (1 - f)
        return rows, columns, pl.multiple_of((1 - f) * 128, 128)

    place = {}
    for n, chunk in enumerate(CHUNKS):
        at = 0
        for i, j, w in chunk:
            place[i, j] = n, pl.ds(at, w)
            at += w

    def products(held_blocks, i, j, w):
        if w == 256:
            return dot(held_blocks[i], held_blocks[j], ((1,), (1,)))
        rows, columns, begin = halved(i, j)
        return dot(held_blocks[rows], held_blocks[columns, pl.ds(begin, 128)], ((1,), (1,)))

    def gram_student(n):
        for i, j, w in CHUNKS[n]:
            gf[n][:, place[i, j][1]] = products(sb, i, j, w)

    def gram(n):
        for i, j, w in CHUNKS[n]:
            part = (gf[n][:, place[i, j][1]] - products(tb, i, j, w)) * scale
            gf[n][:, place[i, j][1]] = part
            gs[n][:, place[i, j][1]] = part.astype(BF16)
        for k in (2, 1, 3):
            rows = pl.multiple_of((x + k) % 4 * 64, 64)
            got["sx", n, k] = copy(gs[n].at[pl.ds(rows, 64)], rx[n].at[k - 1], device(dx=k))

    own_x = pl.multiple_of(x * 64, 64)
    own_y = pl.multiple_of(h * 16, 16)
    own = pl.multiple_of(x * 64 + h * 16, 16)

    def sum_x(n):
        for k in (1, 3, 2):
            got["sx", n, k].wait_recv()
        total = gf[n][pl.ds(own_x, 64)]
        for k in range(3):
            total += rx[n][k].astype(F32)
        xf[n][...] = total
        xs[n][...] = total.astype(BF16)
        for k in (2, 1, 3):
            if n in WHOLE:
                got["sy", n, k] = copy(xs[n], ry[n].at[k - 1], device(dh=k))
            else:
                rows = pl.multiple_of((h + k) % 4 * 16, 16)
                to = ry[n].at[k - 1, pl.ds(0, 16)]
                got["sy", n, k] = copy(xs[n].at[pl.ds(rows, 16)], to, device(dh=k))

    def sum_y(n):
        for k in (1, 3, 2):
            got["sy", n, k].wait_recv()
        if n in WHOLE:
            total = xf[n][...]
            for k in range(3):
                total += ry[n][k].astype(F32)
            gg[n][pl.ds(own_x, 64)] = total.astype(BF16)
            return
        total = xf[n][pl.ds(own_y, 16)]
        for k in range(3):
            total += ry[n][k, pl.ds(0, 16)].astype(F32)
        gg[n][pl.ds(own, 16)] = total.astype(BF16)
        for k in (2, 1, 3):
            piece = gg[n].at[pl.ds(own, 16)]
            got["gy", n, k] = copy(piece, piece, device(dh=k))

    def gather_x(n):
        if n not in WHOLE:
            for k in (1, 3, 2):
                got["gy", n, k].wait_recv()
        for k in (2, 1, 3):
            piece = gg[n].at[pl.ds(own_x, 64)]
            got["gx", n, k] = copy(piece, piece, device(dx=k))

    def arrived(n):
        for k in (1, 3, 2):
            got["gx", n, k].wait_recv()

    for k, to in ((1, device(dz=-1)), (4, device(dl=1))):
        for which in (0, 1):
            first(which, k, to)
    for made in own_copies:
        made.wait()
    gram_student(0)
    gram(0)
    for which in (0, 1):
        first(which, 3, device(dz=1))
    for which in (0, 1):
        forward(which, 1, 2, device(dz=-2))
    gram_student(1)
    gram(1)
    sum_x(0)
    for which in (0, 1):
        forward(which, 3, 5, device(dl=1))
    for which in (0, 1):
        got[which, 4].wait_recv()
    gram_student(2)
    gram(2)
    sum_x(1)
    sum_y(0)
    got[0, 5].wait_recv()
    got[0, 2].wait_recv()
    for n in (4, 5, 3):
        gram_student(n)
    got[1, 2].wait_recv()
    gram(4)
    got[1, 5].wait_recv()
    gram(5)
    gram(3)
    half[...] = jnp.zeros_like(half)
    sum_x(2)
    sum_y(1)
    gather_x(0)
    sum_x(4)
    gather_x(1)
    sum_y(2)
    sum_x(5)
    sum_x(3)
    sum_y(4)
    gather_x(4)
    gather_x(2)
    sum_y(5)
    gather_x(5)
    sum_y(3)
    gather_x(3)
    for n in (0, 1, 2, 4):
        arrived(n)

    def halves(n):
        for i, j, w in CHUNKS[n]:
            if w == 128:
                rows, columns, begin = halved(i, j)
                gap = gg[place[i, j][0]][:, place[i, j][1]]
                half[rows] += dot(gap, sb[columns, pl.ds(begin, 128)], ((1,), (0,)))
                half[columns, pl.ds(begin, 128)] += dot(gap, sb[rows], ((0,), (0,)))

    def gradient(k, chunks):
        total = half[k]
        for n in chunks:
            for i, j, w in CHUNKS[n]:
                if w == 256 and k in (i, j):
                    gap = gg[n][:, place[i, j][1]]
                    if k == i:
                        total = total + dot(gap, sb[j], ((1,), (0,)))
                    else:
                        total = total + dot(gap, sb[i], ((0,), (0,)))
        return total

    def give(k, chunks):
        ps[k - 1] = gradient(k, chunks).astype(BF16)
        got["f", k] = copy(ps.at[k - 1], fr.at[k - 1], device(dl=COVER[k][0], dz=COVER[k][1]))

    halves(2)
    halves(4)
    give(3, (2,))
    for k in (2, 4):
        half[k] = gradient(k, (2, 4))
    arrived(5)
    halves(5)
    give(2, (5,))
    give(4, (5,))
    half[0] = gradient(0, (0, 1, 2, 4))
    half[1] = gradient(1, (1, 2))
    arrived(3)
    give(5, (3,))
    give(1, (3,))
    total = half[0]
    for k in (3, 4, 2, 1, 5):
        got["f", k].wait_recv()
        total += fr[k - 1].astype(F32)
    out_ref[0] = total.astype(BF16)
    for made in pending:
        made.wait_send()


def by_chunk(shape, dtype):
    return tuple(pltpu.VMEM((*shape, w), dtype) for w in WIDTHS)


def body(student, teacher):
    scale = 1.0 / (student.shape[2] * lax.axis_size("row"))
    blocks = pltpu.VMEM((HELD, 256, 256), BF16)
    partials = pltpu.VMEM((HELD - 1, 256, 256), BF16)
    return pl.pallas_call(
        functools.partial(kernel, scale),
        out_shape=jax.ShapeDtypeStruct(student.shape, BF16),
        in_specs=[pl.BlockSpec(memory_space=pl.ANY)] * 2,
        out_specs=pl.BlockSpec(memory_space=pltpu.VMEM),
        scratch_shapes=[
            blocks,
            blocks,
            by_chunk((256,), BF16),
            by_chunk((256,), F32),
            by_chunk((3, 64), BF16),
            by_chunk((64,), BF16),
            by_chunk((64,), F32),
            by_chunk((3, 64), BF16),
            by_chunk((256,), BF16),
            pltpu.VMEM((HELD, 256, 256), F32),
            partials,
            partials,
            pltpu.SemaphoreType.DMA((COPIES,)),
            pltpu.SemaphoreType.DMA((COPIES,)),
            pltpu.SemaphoreType.DMA((2,)),
        ],
        compiler_params=pltpu.CompilerParams(
            collective_id=0, has_side_effects=True, vmem_limit_bytes=55040 * 1024
        ),
    )(student, teacher)


def solution(mesh):
    placed = P("img", "col", "row")
    return jax.shard_map(
        body, mesh=mesh, in_specs=(placed, placed), out_specs=placed, check_vma=False
    )
```
